32 devices in a mesh: dp: 4 (over y, x), shard: 8 (over z, core).
Axes of the slice: x: 2, y: 2, z: 4, core: 2. Of those that a mesh axis runs over, the one named last changes fastest.
Arguments:
- grads: bfloat16 [4, 16, 1024, 1024], P('dp', None, 'shard'), may hold values from -6 to 6
- params: bfloat16 [16, 1024, 1024], P(None, 'shard'), may hold values from -6 to 6
- stats: float32 [4, 8, 1024, 1024], P('dp', 'shard'), may hold values from -1 to 17, as said below
- roots: float32 [4, 8, 1024, 1024], P('dp', 'shard'), may hold values from -1 to 2, as said below
- table: int32 [4, 4], replicated, may hold values from 0 to 3, each once within a row
Outputs:
- new_params: bfloat16 [16, 1024, 1024], P(None, 'shard')
- new_stats: float32 [4, 8, 1024, 1024], P('dp', 'shard')
The draws below stay inside these ranges and needn't reach their ends.
Inputs may be any that keep to these rules, and one draw needn't show every extreme that they name: Each row of table names each of the 4 blocks of its group once. Every matrix stats[d, s] is symmetric. Every matrix roots[d, s] is symmetric.
All inputs are finite; a program needn't handle non-finite values.
Results may differ from the reference program's by a relative error of at most 0.0085.
Values may be sent and summed in bfloat16 or wider, within the bound.
A program may use at most 128 MiB of HBM per device.

```python
import math
import jax
import jax.numpy as jnp
from jax import lax

BS = 1024
NB = 16
N_DP = 4
N_SHARD = 8


def draw_stats(key, part):
    key = jax.random.fold_in(key, 11)
    first_key, second_key = jax.random.split(key)
    shape = (N_DP, N_SHARD, BS, BS)
    diagonal = jnp.exp(jax.random.uniform(first_key, (N_DP, N_SHARD, 1, BS), jnp.float32, 0.0, math.log(10.0)))
    noise = jax.random.normal(second_key, shape, jnp.float32)
    noise = noise * (0.25 / math.sqrt(BS))
    symmetric = noise + jnp.swapaxes(noise, -1, -2)
    return symmetric + jnp.eye(BS, dtype=jnp.float32) * diagonal


def draw_roots(key, part):
    key = jax.random.fold_in(key, 23)
    first_key, second_key = jax.random.split(key)
    shape = (N_DP, N_SHARD, BS, BS)
    diagonal = jnp.exp(jax.random.uniform(first_key, (N_DP, N_SHARD, 1, BS), jnp.float32, math.log(0.25), math.log(1.0)))
    noise = jax.random.normal(second_key, shape, jnp.float32)
    noise = noise * (0.1 / math.sqrt(BS))
    symmetric = noise + jnp.swapaxes(noise, -1, -2)
    return symmetric + jnp.eye(BS, dtype=jnp.float32) * diagonal


def with_spikes(array, rng, source, target, shards_of, factor):
    owner, partner = [(jnp.arange(array.shape[position]) // (array.shape[position] // shards_of)).reshape([-1 if axis == position else 1 for axis in range(array.ndim)]) for position in (source, target)]
    chosen = jax.random.permutation(rng, shards_of)[partner]
    strong = (owner == chosen) | (owner == (partner + shards_of // 2) % shards_of)
    return jnp.where(strong, factor * array, array)


def steps_of(own_key, shape, shards, least, high):
    def one(dim, blocks):
        steps = jax.random.uniform(jax.random.fold_in(jax.random.fold_in(own_key, 6), dim), (blocks,), jnp.float32, least / len(shards), high / len(shards))
        return jnp.repeat(jnp.exp(steps), shape[dim] // blocks).reshape((-1,) + (1,) * (len(shape) - dim - 1))

    loudness = one(*shards[0])
    for cut in shards[1:]:
        loudness = loudness * one(*cut)
    return loudness


def centred(key, dims, width, bound, pieces=(), held_as=jnp.bfloat16):
    drawn = jax.random.normal(key, dims, jnp.float32) * width
    if len(pieces) > 0:
        drawn = steps_of(key, dims, pieces, -0.22, 0.18) * drawn
    return jnp.clip(drawn, min=-bound, max=bound).astype(held_as)


def heavy_noise(rng, shape, scale, bound, pieces, heavy, held_as=jnp.bfloat16):
    result = scale * jax.random.normal(rng, shape, jnp.float32)
    if pieces:
        result = result * steps_of(rng, shape, pieces, -0.22, 0.18)
    return jnp.clip(with_spikes(result, jax.random.fold_in(rng, 3), *heavy), -bound, bound).astype(held_as)


def setup_inputs(seed: int = 0) -> dict:
    arg_keys = jax.random.split(jax.random.key(seed), 6)
    grads = heavy_noise(arg_keys[0], (N_DP, NB, BS, BS), 1.0, 6.0, ((0, 4), (2, 8)), (0, 1, 4, 2.0))
    params = centred(arg_keys[1], (NB, BS, BS), 1.0, 6.0, ((1, 8),))
    stats = draw_stats(jax.random.fold_in(arg_keys[5], 71), 0)
    roots = draw_roots(jax.random.fold_in(arg_keys[5], 71), 0)
    table = jax.vmap(lambda own: jax.random.permutation(own, N_SHARD // 2))(jax.random.split(arg_keys[4], N_DP)).reshape((N_DP, N_SHARD // 2)).astype(jnp.int32)
    return dict(grads=grads, params=params, stats=stats, roots=roots, table=table)


keep_rate = 0.75
step_size = 0.25


def reference(grads, params, stats, roots, table):
    summed = jnp.sum(grads.astype(jnp.float32), axis=0).astype(jnp.bfloat16)
    row_blocks = NB // N_DP
    owners = (jnp.arange(N_DP, dtype=jnp.int32)[:, None] * row_blocks + table.astype(jnp.int32)).reshape(-1).astype(jnp.int32)
    pair_stats = stats.reshape(NB, 2, BS, BS)
    pair_roots = roots.reshape(NB, 2, BS, BS)

    def per_pair(item):
        block_id, stat_pair, root_pair = item
        gradient = lax.dynamic_index_in_dim(summed, block_id, 0, keepdims=False)
        left_gram = jnp.dot(gradient, gradient.T, preferred_element_type=jnp.float32)
        right_gram = jnp.dot(gradient.T, gradient, preferred_element_type=jnp.float32)
        new_left = keep_rate * stat_pair[0] + ((1.0 - keep_rate) / BS) * left_gram
        new_right = keep_rate * stat_pair[1] + ((1.0 - keep_rate) / BS) * right_gram
        first = jnp.dot(root_pair[0], gradient.astype(jnp.float32), precision=lax.Precision.HIGHEST)
        update = jnp.dot(first, root_pair[1], precision=lax.Precision.HIGHEST)
        return jnp.stack([new_left, new_right]), update

    new_stats, updates = lax.map(per_pair, (owners, pair_stats, pair_roots))
    ordered = jnp.zeros((NB, BS, BS), jnp.float32).at[owners].set(updates)
    new_params = (params.astype(jnp.float32) - step_size * ordered).astype(jnp.bfloat16)
    return new_params, new_stats.reshape(N_DP, N_SHARD, BS, BS)
```

```python
import functools

import jax
import jax.numpy as jnp
from jax import lax
from jax.experimental import pallas as pl
from jax.experimental.pallas import tpu as pltpu
from jax.sharding import PartitionSpec as P

keep_rate = 0.75
step_size = 0.25
SUB = 16
AHEAD = 4
LAG = 2


def remote(src, dst, sems, index, **device):
    send_sem, recv_sem = sems
    return pltpu.make_async_remote_copy(
        src_ref=src,
        dst_ref=dst,
        send_sem=send_sem.at[index],
        recv_sem=recv_sem.at[index],
        device_id=device,
        device_id_type=pl.DeviceIdType.MESH,
    )


def exchange_kernel(pairs, blocks, rows, size, *refs):
    refs = list(refs)
    table, grads, roots, update_out, gram_out = refs[:5]
    refs = refs[5:]
    chunks = rows // SUB
    rounds = chunks // 2
    first_own = [refs.pop(0) for _ in range(chunks)]
    second_own = [refs.pop(0) for _ in range(chunks)]
    (first_pass, partial, mine, mine_x, mine_y, outgoing, gradient, root_f32, factors, left_rows, updates, gram) = refs[:12]
    sems = refs[12:]
    first_sems, second_sems, block_sems, core_sems, factor_sems, row_sems, gather_sems, relay_sems = [
        (sems[2 * n], sems[2 * n + 1]) for n in range(8)
    ]
    local_sem, gram_sem = sems[16:18]

    d = lax.axis_index("dp")
    s = lax.axis_index("shard")
    pair = s // 2
    core = s % 2
    other = 2 * pair + 1 - core
    d_x = d + 1 - 2 * (d % 2)
    d_y = (d + 2) % 4
    d_z = 3 - d

    def ahead(k):
        return (pair + k) % pairs

    def behind(k):
        return (pair + pairs - k) % pairs

    barrier = pltpu.get_barrier_semaphore()
    greeted = [dict(dp=d_x, shard=s), dict(dp=d_y, shard=s), dict(dp=d, shard=other)]
    greeted += [dict(dp=d, shard=2 * ahead(k) + core) for k in range(1, pairs)]
    for device in greeted:
        pl.semaphore_signal(barrier, inc=1, device_id=device, device_id_type=pl.DeviceIdType.MESH)
    pl.semaphore_wait(barrier, len(greeted))

    sent = []

    def start(copy):
        copy.start()
        sent.append(copy)
        return copy

    def group(owner, i):
        return grads.at[0, pl.ds(owner * blocks, blocks), pl.ds(i * SUB, SUB), :]

    def first_copies(i):
        near = d_x if i % 2 == 0 else d_y
        return [
            remote(group(near, i), first_own[i], first_sems, (i, 0), dp=near, shard=s),
            remote(group(d_z, i), first_pass.at[i], first_sems, (i, 1), dp=near, shard=s),
        ]

    def start_first(i):
        for copy in first_copies(i)[::-1]:
            start(copy)

    for i in range(min(AHEAD, chunks)):
        start_first(i)
    loads = [
        pltpu.make_async_copy(roots.at[0, 0], root_f32, local_sem.at[0]),
        pltpu.make_async_copy(grads.at[0, pl.ds(d_y * blocks, blocks)], mine_y, local_sem.at[1]),
        pltpu.make_async_copy(grads.at[0, pl.ds(d_x * blocks, blocks)], mine_x, local_sem.at[2]),
        pltpu.make_async_copy(grads.at[0, pl.ds(d * blocks, blocks)], mine, local_sem.at[3]),
    ]
    for copy in loads:
        copy.start()
    loads[0].wait()
    factors[core] = root_f32[...].astype(jnp.bfloat16)
    start(remote(factors.at[core], factors.at[core], factor_sems, 0, dp=d, shard=other))
    for copy in loads[1:]:
        copy.wait()

    def second_copy(i):
        far = d_y if i % 2 == 0 else d_x
        return remote(partial.at[i], second_own[i], second_sems, i, dp=far, shard=s)

    def pass_on(i):
        for copy in first_copies(i):
            copy.wait_recv()
        if i + AHEAD < chunks:
            start_first(i + AHEAD)
        held = mine_y if i % 2 == 0 else mine_x
        for b in range(blocks):
            total = held[b, pl.ds(i * SUB, SUB), :].astype(jnp.float32) + first_pass[i, b].astype(jnp.float32)
            partial[i, b] = total.astype(jnp.bfloat16)
        start(second_copy(i))

    def finish_sum(i):
        second_copy(i).wait_recv()
        for k in range(pairs):
            b = table[d, ahead(k)]
            total = mine[b, pl.ds(i * SUB, SUB), :].astype(jnp.float32) + first_own[i][b].astype(jnp.float32)
            total = (total + second_own[i][b].astype(jnp.float32)).astype(jnp.bfloat16)
            if k == 0:
                gradient[pl.ds(pl.multiple_of(s * rows + i * SUB, SUB), SUB), :] = total
            else:
                outgoing[i // 2, k - 1, pl.ds(i % 2 * SUB, SUB), :] = total

    def gradient_rows(owner, m):
        return gradient.at[pl.ds(pl.multiple_of(owner * rows + m * 2 * SUB, 2 * SUB), 2 * SUB), :]

    def block_copy(m, k):
        return remote(
            outgoing.at[m, k - 1],
            gradient_rows(s, m),
            block_sems,
            (m, k - 1),
            dp=d,
            shard=2 * ahead(k) + core,
        )

    def core_copy(m, k, owner):
        return remote(gradient_rows(owner, m), gradient_rows(owner, m), core_sems, (m, k), dp=d, shard=other)

    def start_blocks(m):
        for k in range(1, pairs):
            start(block_copy(m, k))
        start(core_copy(m, 0, s))

    def relay_blocks(m):
        for k in range(1, pairs):
            sender = 2 * behind(k) + core
            remote(outgoing.at[m, k - 1], gradient_rows(sender, m), block_sems, (m, k - 1), dp=d, shard=other).wait_recv()
            start(core_copy(m, k, sender))

    for i in range(chunks + LAG):
        if i < chunks:
            pass_on(i)
        j = i - LAG
        if j >= 0:
            finish_sum(j)
            if j % 2 == 1:
                start_blocks(j // 2)
                if j // 2 >= 1:
                    relay_blocks(j // 2 - 1)

    order = [0, pairs // 2] + [k for k in range(1, pairs) if k != pairs // 2]
    remote(factors.at[core], factors.at[1 - core], factor_sems, 0, dp=d, shard=other).wait_recv()
    for n, k in enumerate(order):
        place = pl.multiple_of((2 * ahead(k) + core) * rows, rows)
        left_rows[pl.ds(n * rows, rows), :] = factors[0, pl.ds(place, rows), :]
    relay_blocks(rounds - 1)
    for m in range(rounds):
        for k in range(pairs):
            core_copy(m, k, 2 * behind(k) + 1 - core).wait_recv()

    def slot(replica, owner):
        return update_out.at[replica * pairs + owner]

    def gather_copies(k, source):
        q = behind(k)
        return [
            remote(source, slot(d, q), gather_sems, (k, 0), dp=d_x, shard=s),
            remote(source, slot(d, q), gather_sems, (k, 1), dp=d_y, shard=s),
        ]

    half = rows // 2

    def part(replica, k, side):
        return slot(replica, behind(k)).at[pl.ds(side * half, half), :]

    def relay_copies(k):
        return [
            remote(part(d_x, k, 0), part(d_x, k, 0), relay_sems, (k, 0), dp=d_y, shard=s),
            remote(part(d_y, k, 1), part(d_y, k, 1), relay_sems, (k, 1), dp=d_x, shard=s),
        ]

    def relay_updates(k):
        q = behind(k)
        relays = relay_copies(k)
        for side, replica in enumerate((d_x, d_y)):
            remote(slot(replica, q), slot(replica, q), gather_sems, (k, side), dp=d_x, shard=s).wait_recv()
            start(relays[side])

    per_step = max(1, min(pairs, 256 // rows))
    for step in range(pairs // per_step):
        base = step * per_step
        one_sided = jnp.dot(
            left_rows[pl.ds(base * rows, per_step * rows), :], gradient[...], preferred_element_type=jnp.float32
        ).astype(jnp.bfloat16)
        both = jnp.dot(one_sided, factors[1], preferred_element_type=jnp.float32).astype(jnp.bfloat16)
        for n in range(base, base + per_step):
            updates[n] = both[(n - base) * rows : (n - base + 1) * rows]
            k = order[n]
            if k == 0:
                for copy in gather_copies(0, updates.at[n]):
                    start(copy)
                own_copy = pltpu.make_async_copy(updates.at[n], slot(d, pair), local_sem.at[4])
                own_copy.start()
            else:
                start(remote(updates.at[n], slot(d, pair), row_sems, k - 1, dp=d, shard=2 * ahead(k) + core))

    tile = min(256, size)
    gram_copies = []

    def gram_tile(n):
        window = pl.ds(n * tile, tile)
        scale = (1.0 - keep_rate) / size

        @pl.when(core == 0)
        def _():
            product = lax.dot_general(
                gradient[window, :], gradient[...], (((1,), (1,)), ((), ())), preferred_element_type=jnp.float32
            )
            gram[window, :] = (scale * product).astype(jnp.bfloat16)

        @pl.when(core == 1)
        def _():
            product = jnp.dot(gradient[:, window].T, gradient[...], preferred_element_type=jnp.float32)
            gram[window, :] = (scale * product).astype(jnp.bfloat16)

        copy = pltpu.make_async_copy(gram.at[window, :], gram_out.at[window, :], gram_sem.at[n])
        copy.start()
        gram_copies.append(copy)

    tiles = list(range(size // tile))
    for n, k in enumerate(order[1:]):
        remote(updates.at[0], slot(d, behind(k)), row_sems, k - 1, dp=d, shard=other).wait_recv()
        for copy in gather_copies(k, slot(d, behind(k))):
            start(copy)
        relay_updates(order[n])
        if tiles:
            gram_tile(tiles.pop(0))
    relay_updates(order[-1])
    while tiles:
        gram_tile(tiles.pop(0))
    for k in order:
        for side in range(2):
            remote(part(d_z, k, side), part(d_z, k, side), relay_sems, (k, side), dp=d_x, shard=s).wait_recv()
    own_copy.wait()
    for copy in gram_copies:
        copy.wait()
    for copy in sent:
        copy.wait_send()


def exchange(table, grads, roots, pairs):
    _, total, rows, size = grads.shape
    blocks = total // 4
    chunks = rows // SUB
    rounds = chunks // 2
    half = jnp.bfloat16
    dma = pltpu.SemaphoreType.DMA
    scratch = [pltpu.VMEM((blocks, SUB, size), half) for _ in range(2 * chunks)]
    scratch += [
        pltpu.VMEM((chunks, blocks, SUB, size), half),
        pltpu.VMEM((chunks, blocks, SUB, size), half),
        pltpu.VMEM((blocks, rows, size), half),
        pltpu.VMEM((blocks, rows, size), half),
        pltpu.VMEM((blocks, rows, size), half),
        pltpu.VMEM((rounds, pairs - 1, 2 * SUB, size), half),
        pltpu.VMEM((size, size), half),
        pltpu.VMEM((size, size), jnp.float32),
        pltpu.VMEM((2, size, size), half),
        pltpu.VMEM((pairs * rows, size), half),
        pltpu.VMEM((pairs, rows, size), half),
        pltpu.VMEM((size, size), half),
    ]
    shapes = [(chunks, 2), (chunks,), (rounds, pairs - 1), (rounds, pairs), (1,), (pairs - 1,), (pairs, 2), (pairs, 2)]
    for shape in shapes:
        scratch += [dma(shape), dma(shape)]
    scratch += [dma((5,)), dma((max(1, size // 256),))]
    return pl.pallas_call(
        functools.partial(exchange_kernel, pairs, blocks, rows, size),
        out_shape=(
            jax.ShapeDtypeStruct((total, rows, size), half),
            jax.ShapeDtypeStruct((size, size), half),
        ),
        in_specs=[
            pl.BlockSpec(memory_space=pltpu.SMEM),
            pl.BlockSpec(memory_space=pl.ANY),
            pl.BlockSpec(memory_space=pl.ANY),
        ],
        out_specs=[pl.BlockSpec(memory_space=pl.ANY)] * 2,
        scratch_shapes=scratch,
        compiler_params=pltpu.CompilerParams(
            collective_id=0, has_side_effects=True, vmem_limit_bytes=44 * 1024 * 1024
        ),
    )(table, grads, roots)


def finish_kernel(table, params, update, stats, gram, new_params, new_stats):
    new_params[...] = (params[...].astype(jnp.float32) - step_size * update[...].astype(jnp.float32)).astype(jnp.bfloat16)
    new_stats[...] = keep_rate * stats[...] + gram[...].astype(jnp.float32)


def finish(table, params, update, stats, gram, pairs):
    total, rows, size = params.shape
    blocks = total // 4
    depth = size // total

    def slot(b, table):
        d, place = b // blocks, b % blocks
        found = 0
        for p in range(pairs):
            found = found + jnp.where(table[d, p] == place, p, 0)
        return d * pairs + found, 0, 0

    whole = pl.BlockSpec((1, rows, size), lambda b, table: (b, 0, 0))
    stripe = pl.BlockSpec((depth, size), lambda b, table: (b, 0))
    return pl.pallas_call(
        finish_kernel,
        grid_spec=pltpu.PrefetchScalarGridSpec(
            num_scalar_prefetch=1,
            grid=(total,),
            in_specs=[whole, pl.BlockSpec((1, rows, size), slot), stripe, stripe],
            out_specs=[whole, stripe],
        ),
        out_shape=(
            jax.ShapeDtypeStruct(params.shape, jnp.bfloat16),
            jax.ShapeDtypeStruct(stats.shape, jnp.float32),
        ),
    )(table, params, update, stats, gram)


def on_device(grads, params, stats, roots, table):
    pairs = lax.axis_size("shard") // 2
    update, gram = exchange(table, grads, roots, pairs)
    new_params, new_stats = finish(table, params, update, stats[0, 0], gram, pairs)
    return new_params, new_stats[None, None]


def solution(mesh):
    placed = (
        P("dp", None, "shard", None),
        P(None, "shard", None),
        P("dp", "shard", None, None),
        P("dp", "shard", None, None),
        P(),
    )
    return jax.shard_map(
        on_device,
        mesh=mesh,
        in_specs=placed,
        out_specs=(P(None, "shard", None), P("dp", "shard", None, None)),
        check_vma=False,
    )
```

```python
import functools

import jax
import jax.numpy as jnp
from jax import lax
from jax.experimental import pallas as pl
from jax.experimental.pallas import tpu as pltpu
from jax.sharding import PartitionSpec as P

keep_rate = 0.75
step_size = 0.25
SUB = 16
AHEAD = 4
LAG = 2
PIECE = 2 * SUB
ROWS_AHEAD = 2


def remote(src, dst, sems, index, **device):
    send_sem, recv_sem = sems
    return pltpu.make_async_remote_copy(
        src_ref=src,
        dst_ref=dst,
        send_sem=send_sem.at[index],
        recv_sem=recv_sem.at[index],
        device_id=device,
        device_id_type=pl.DeviceIdType.MESH,
    )


def exchange_kernel(pairs, blocks, rows, size, *refs):
    refs = list(refs)
    table, grads, roots, update_out, gram_out = refs[:5]
    refs = refs[5:]
    chunks = rows // SUB
    rounds = chunks // 2
    pieces = rows // PIECE
    half = PIECE // 2
    first_own = [refs.pop(0) for _ in range(chunks)]
    second_own = [refs.pop(0) for _ in range(chunks)]
    (first_pass, partial, mine, mine_x, mine_y, outgoing, gradient, root_f32, factors, left_rows, updates, gram) = refs[:12]
    sems = refs[12:]
    first_sems, second_sems, block_sems, core_sems, factor_sems, row_sems, gather_sems, relay_sems = [
        (sems[2 * n], sems[2 * n + 1]) for n in range(8)
    ]
    local_sem, gram_sem = sems[16:18]

    d = lax.axis_index("dp")
    s = lax.axis_index("shard")
    pair = s // 2
    core = s % 2
    other = 2 * pair + 1 - core
    d_x = d + 1 - 2 * (d % 2)
    d_y = (d + 2) % 4
    d_z = 3 - d

    def ahead(k):
        return (pair + k) % pairs

    def behind(k):
        return (pair + pairs - k) % pairs

    barrier = pltpu.get_barrier_semaphore()
    greeted = [dict(dp=d_x, shard=s), dict(dp=d_y, shard=s), dict(dp=d, shard=other)]
    greeted += [dict(dp=d, shard=2 * ahead(k) + core) for k in range(1, pairs)]
    for device in greeted:
        pl.semaphore_signal(barrier, inc=1, device_id=device, device_id_type=pl.DeviceIdType.MESH)
    pl.semaphore_wait(barrier, len(greeted))

    sent = []

    def start(copy):
        copy.start()
        sent.append(copy)
        return copy

    def group(owner, i):
        return grads.at[0, pl.ds(owner * blocks, blocks), pl.ds(i * SUB, SUB), :]

    def first_copies(i):
        near = d_x if i % 2 == 0 else d_y
        return [
            remote(group(near, i), first_own[i], first_sems, (i, 0), dp=near, shard=s),
            remote(group(d_z, i), first_pass.at[i], first_sems, (i, 1), dp=near, shard=s),
        ]

    def start_first(i):
        for copy in first_copies(i)[::-1]:
            start(copy)

    for i in range(min(AHEAD, chunks)):
        start_first(i)
    loads = [
        pltpu.make_async_copy(roots.at[0, 0], root_f32, local_sem.at[0]),
        pltpu.make_async_copy(grads.at[0, pl.ds(d_y * blocks, blocks)], mine_y, local_sem.at[1]),
        pltpu.make_async_copy(grads.at[0, pl.ds(d_x * blocks, blocks)], mine_x, local_sem.at[2]),
        pltpu.make_async_copy(grads.at[0, pl.ds(d * blocks, blocks)], mine, local_sem.at[3]),
    ]
    for copy in loads:
        copy.start()
    loads[0].wait()
    factors[core] = root_f32[...].astype(jnp.bfloat16)
    start(remote(factors.at[core], factors.at[core], factor_sems, 0, dp=d, shard=other))
    for copy in loads[1:]:
        copy.wait()

    def second_copy(i):
        far = d_y if i % 2 == 0 else d_x
        return remote(partial.at[i], second_own[i], second_sems, i, dp=far, shard=s)

    def pass_on(i):
        for copy in first_copies(i):
            copy.wait_recv()
        if i + AHEAD < chunks:
            start_first(i + AHEAD)
        held = mine_y if i % 2 == 0 else mine_x
        for b in range(blocks):
            total = held[b, pl.ds(i * SUB, SUB), :].astype(jnp.float32) + first_pass[i, b].astype(jnp.float32)
            partial[i, b] = total.astype(jnp.bfloat16)
        start(second_copy(i))

    def finish_sum(i):
        second_copy(i).wait_recv()
        for k in range(pairs):
            b = table[d, ahead(k)]
            total = mine[b, pl.ds(i * SUB, SUB), :].astype(jnp.float32) + first_own[i][b].astype(jnp.float32)
            total = (total + second_own[i][b].astype(jnp.float32)).astype(jnp.bfloat16)
            if k == 0:
                gradient[pl.ds(pl.multiple_of(s * rows + i * SUB, SUB), SUB), :] = total
            else:
                outgoing[i // 2, k - 1, pl.ds(i % 2 * SUB, SUB), :] = total

    def gradient_rows(owner, m):
        return gradient.at[pl.ds(pl.multiple_of(owner * rows + m * 2 * SUB, 2 * SUB), 2 * SUB), :]

    def block_copy(m, k):
        return remote(
            outgoing.at[m, k - 1],
            gradient_rows(s, m),
            block_sems,
            (m, k - 1),
            dp=d,
            shard=2 * ahead(k) + core,
        )

    def core_copy(m, k, owner):
        return remote(gradient_rows(owner, m), gradient_rows(owner, m), core_sems, (m, k), dp=d, shard=other)

    def start_blocks(m):
        for k in range(1, pairs):
            start(block_copy(m, k))
        start(core_copy(m, 0, s))

    def relay_blocks(m):
        for k in range(1, pairs):
            sender = 2 * behind(k) + core
            remote(outgoing.at[m, k - 1], gradient_rows(sender, m), block_sems, (m, k - 1), dp=d, shard=other).wait_recv()
            start(core_copy(m, k, sender))

    for i in range(chunks + LAG):
        if i < chunks:
            pass_on(i)
        j = i - LAG
        if j >= 0:
            finish_sum(j)
            if j % 2 == 1:
                start_blocks(j // 2)
                if j // 2 >= 1:
                    relay_blocks(j // 2 - 1)

    order = [0, pairs // 2] + [k for k in range(1, pairs) if k != pairs // 2]
    remote(factors.at[core], factors.at[1 - core], factor_sems, 0, dp=d, shard=other).wait_recv()
    for h in range(pieces):
        for n, k in enumerate(order):
            place = pl.multiple_of((2 * ahead(k) + core) * rows + h * PIECE, PIECE)
            left_rows[pl.ds((h * pairs + n) * PIECE, PIECE), :] = factors[0, pl.ds(place, PIECE), :]
    relay_blocks(rounds - 1)
    for m in range(rounds):
        for k in range(pairs):
            core_copy(m, k, 2 * behind(k) + 1 - core).wait_recv()

    def slot(replica, owner, h):
        return update_out.at[replica * pairs + owner, pl.ds(h * PIECE, PIECE), :]

    def start_gather(h, k, source):
        q = behind(k)
        start(remote(source, slot(d, q, h), gather_sems, (h, k, 0), dp=d_x, shard=s))
        start(remote(source, slot(d, q, h), gather_sems, (h, k, 1), dp=d_y, shard=s))

    def part(replica, k, h, side):
        return update_out.at[replica * pairs + behind(k), pl.ds(h * PIECE + side * half, half), :]

    def relay_updates(h, k):
        q = behind(k)
        for side, replica, to in ((0, d_x, d_y), (1, d_y, d_x)):
            remote(slot(replica, q, h), slot(replica, q, h), gather_sems, (h, k, side), dp=to, shard=s).wait_recv()
            mine_part = part(replica, k, h, side)
            start(remote(mine_part, mine_part, relay_sems, (h, k, side), dp=to, shard=s))

    def start_rows(h):
        for n, k in list(enumerate(order))[1:]:
            device = dict(dp=d, shard=2 * ahead(k) + core)
            start(remote(updates.at[h, n], slot(d, pair, h), row_sems, (h, k - 1), **device))

    per_step = max(1, min(pieces, 256 // (pairs * PIECE)))
    depth = pairs * PIECE
    own_copies = []
    for base in range(0, pieces, per_step):
        one_sided = jnp.dot(
            left_rows[pl.ds(base * depth, per_step * depth), :], gradient[...], preferred_element_type=jnp.float32
        ).astype(jnp.bfloat16)
        both = jnp.dot(one_sided, factors[1], preferred_element_type=jnp.float32).astype(jnp.bfloat16)
        for h in range(base, base + per_step):
            for n in range(pairs):
                place = ((h - base) * pairs + n) * PIECE
                updates[h, n] = both[place : place + PIECE]
            if h < ROWS_AHEAD:
                start_rows(h)
            start_gather(h, 0, updates.at[h, 0])
            own_copies.append(pltpu.make_async_copy(updates.at[h, 0], slot(d, pair, h), local_sem.at[4 + h]))
            own_copies[-1].start()

    tile = min(256, size)
    gram_copies = []

    def gram_tile(n):
        window = pl.ds(n * tile, tile)
        scale = (1.0 - keep_rate) / size

        @pl.when(core == 0)
        def _():
            product = lax.dot_general(
                gradient[window, :], gradient[...], (((1,), (1,)), ((), ())), preferred_element_type=jnp.float32
            )
            gram[window, :] = (scale * product).astype(jnp.bfloat16)

        @pl.when(core == 1)
        def _():
            product = jnp.dot(gradient[:, window].T, gradient[...], preferred_element_type=jnp.float32)
            gram[window, :] = (scale * product).astype(jnp.bfloat16)

        copy = pltpu.make_async_copy(gram.at[window, :], gram_out.at[window, :], gram_sem.at[n])
        copy.start()
        gram_copies.append(copy)

    tiles = list(range(size // tile))
    for h in range(pieces):
        for k in order[1:]:
            remote(updates.at[h, 0], slot(d, behind(k), h), row_sems, (h, k - 1), dp=d, shard=other).wait_recv()
            start_gather(h, k, slot(d, behind(k), h))
        if h + ROWS_AHEAD < pieces:
            start_rows(h + ROWS_AHEAD)
        relay_updates(h, 0)
        if h >= 1:
            for k in order[1:]:
                relay_updates(h - 1, k)
        if tiles:
            gram_tile(tiles.pop(0))
    for k in order[1:]:
        relay_updates(pieces - 1, k)
    while tiles:
        gram_tile(tiles.pop(0))
    for h in range(pieces):
        for k in order:
            for side in range(2):
                far = part(d_z, k, h, side)
                remote(far, far, relay_sems, (h, k, side), dp=d_x, shard=s).wait_recv()
    for copy in own_copies:
        copy.wait()
    for copy in gram_copies:
        copy.wait()
    for copy in sent:
        copy.wait_send()


def exchange(table, grads, roots, pairs):
    _, total, rows, size = grads.shape
    blocks = total // 4
    chunks = rows // SUB
    rounds = chunks // 2
    pieces = rows // PIECE
    half = jnp.bfloat16
    dma = pltpu.SemaphoreType.DMA
    scratch = [pltpu.VMEM((blocks, SUB, size), half) for _ in range(2 * chunks)]
    scratch += [
        pltpu.VMEM((chunks, blocks, SUB, size), half),
        pltpu.VMEM((chunks, blocks, SUB, size), half),
        pltpu.VMEM((blocks, rows, size), half),
        pltpu.VMEM((blocks, rows, size), half),
        pltpu.VMEM((blocks, rows, size), half),
        pltpu.VMEM((rounds, pairs - 1, 2 * SUB, size), half),
        pltpu.VMEM((size, size), half),
        pltpu.VMEM((size, size), jnp.float32),
        pltpu.VMEM((2, size, size), half),
        pltpu.VMEM((pairs * rows, size), half),
        pltpu.VMEM((pieces, pairs, PIECE, size), half),
        pltpu.VMEM((size, size), half),
    ]
    shapes = [(chunks, 2), (chunks,), (rounds, pairs - 1), (rounds, pairs), (1,)]
    shapes += [(pieces, pairs - 1), (pieces, pairs, 2), (pieces, pairs, 2)]
    for shape in shapes:
        scratch += [dma(shape), dma(shape)]
    scratch += [dma((4 + pieces,)), dma((max(1, size // 256),))]
    return pl.pallas_call(
        functools.partial(exchange_kernel, pairs, blocks, rows, size),
        out_shape=(
            jax.ShapeDtypeStruct((total, rows, size), half),
            jax.ShapeDtypeStruct((size, size), half),
        ),
        in_specs=[
            pl.BlockSpec(memory_space=pltpu.SMEM),
            pl.BlockSpec(memory_space=pltpu.HBM),
            pl.BlockSpec(memory_space=pltpu.HBM),
        ],
        out_specs=[pl.BlockSpec(memory_space=pl.ANY)] * 2,
        scratch_shapes=scratch,
        compiler_params=pltpu.CompilerParams(
            collective_id=0, has_side_effects=True, vmem_limit_bytes=44 * 1024 * 1024
        ),
    )(table, grads, roots)


def finish_kernel(pairs, table, params, update, stats, gram, params_out, stats_out, new_params, new_stats, sems):
    total = params.shape[0]
    blocks = total // 4
    depth = stats.shape[0] // total
    copies = []
    for b in range(total):
        d, place = b // blocks, b % blocks
        found = jnp.int32(d * pairs)
        for p in range(pairs):
            found = found + jnp.where(table[d, p] == place, p, 0)
        stripe = pl.ds(b * depth, depth)
        new_stats[stripe, :] = keep_rate * stats[stripe, :] + gram[stripe, :].astype(jnp.float32)
        copies.append(pltpu.make_async_copy(new_stats.at[stripe, :], stats_out.at[stripe, :], sems.at[0, b]))
        copies[-1].start()
        moved = params[b].astype(jnp.float32) - step_size * update[found].astype(jnp.float32)
        new_params[b] = moved.astype(jnp.bfloat16)
        copies.append(pltpu.make_async_copy(new_params.at[b], params_out.at[b], sems.at[1, b]))
        copies[-1].start()
    for copy in copies:
        copy.wait()


def finish(table, params, update, stats, gram, pairs):
    return pl.pallas_call(
        functools.partial(finish_kernel, pairs),
        in_specs=[pl.BlockSpec(memory_space=pltpu.SMEM)] + [pl.BlockSpec(memory_space=pltpu.VMEM)] * 4,
        out_specs=[pl.BlockSpec(memory_space=pl.ANY)] * 2,
        out_shape=(
            jax.ShapeDtypeStruct(params.shape, jnp.bfloat16),
            jax.ShapeDtypeStruct(stats.shape, jnp.float32),
        ),
        scratch_shapes=[
            pltpu.VMEM(params.shape, jnp.bfloat16),
            pltpu.VMEM(stats.shape, jnp.float32),
            pltpu.SemaphoreType.DMA((2, params.shape[0])),
        ],
        compiler_params=pltpu.CompilerParams(vmem_limit_bytes=32 * 1024 * 1024),
    )(table, params, update, stats, gram)


def on_device(grads, params, stats, roots, table):
    pairs = lax.axis_size("shard") // 2
    update, gram = exchange(table, grads, roots, pairs)
    new_params, new_stats = finish(table, params, update, stats[0, 0], gram, pairs)
    return new_params, new_stats[None, None]


def solution(mesh):
    placed = (
        P("dp", None, "shard", None),
        P(None, "shard", None),
        P("dp", "shard", None, None),
        P("dp", "shard", None, None),
        P(),
    )
    return jax.shard_map(
        on_device,
        mesh=mesh,
        in_specs=placed,
        out_specs=(P(None, "shard", None), P("dp", "shard", None, None)),
        check_vma=False,
    )
```

```python
import functools

import jax
import jax.numpy as jnp
from jax import lax
from jax.experimental import pallas as pl
from jax.experimental.pallas import tpu as pltpu
from jax.sharding import PartitionSpec as P

keep_rate = 0.75
step_size = 0.25
SUB = 16
AHEAD = 4
LAG = 3
PIECE = 2 * SUB
ROWS_AHEAD = 3


def remote(src, dst, sems, index, **device):
    send_sem, recv_sem = sems
    return pltpu.make_async_remote_copy(
        src_ref=src,
        dst_ref=dst,
        send_sem=send_sem.at[index],
        recv_sem=recv_sem.at[index],
        device_id=device,
        device_id_type=pl.DeviceIdType.MESH,
    )


def exchange_kernel(pairs, blocks, rows, size, *refs):
    refs = list(refs)
    table, grads, roots, update_out, gram_out = refs[:5]
    refs = refs[5:]
    chunks = rows // SUB
    rounds = chunks // 2
    pieces = rows // PIECE
    half = PIECE // 2
    first_own = [refs.pop(0) for _ in range(chunks)]
    second_own = [refs.pop(0) for _ in range(chunks)]
    (first_pass, partial, mine, mine_x, mine_y, outgoing, gradient, root_f32, factors, left_rows, updates, gram) = refs[:12]
    sems = refs[12:]
    first_sems, second_sems, block_sems, core_sems, factor_sems, row_sems, gather_sems, relay_sems = [
        (sems[2 * n], sems[2 * n + 1]) for n in range(8)
    ]
    local_sem, gram_sem = sems[16:18]

    d = lax.axis_index("dp")
    s = lax.axis_index("shard")
    pair = s // 2
    core = s % 2
    other = 2 * pair + 1 - core
    d_x = d + 1 - 2 * (d % 2)
    d_y = (d + 2) % 4
    d_z = 3 - d

    def ahead(k):
        return (pair + k) % pairs

    def behind(k):
        return (pair + pairs - k) % pairs

    barrier = pltpu.get_barrier_semaphore()
    greeted = [dict(dp=d_x, shard=s), dict(dp=d_y, shard=s), dict(dp=d, shard=other)]
    greeted += [dict(dp=d, shard=2 * ahead(k) + core) for k in range(1, pairs)]
    for device in greeted:
        pl.semaphore_signal(barrier, inc=1, device_id=device, device_id_type=pl.DeviceIdType.MESH)
    pl.semaphore_wait(barrier, len(greeted))

    sent = []

    def start(copy):
        copy.start()
        sent.append(copy)
        return copy

    def group(owner, i):
        return grads.at[0, pl.ds(owner * blocks, blocks), pl.ds(i * SUB, SUB), :]

    def first_copies(i):
        near = d_x if i % 2 == 0 else d_y
        return [
            remote(group(near, i), first_own[i], first_sems, (i, 0), dp=near, shard=s),
            remote(group(d_z, i), first_pass.at[i], first_sems, (i, 1), dp=near, shard=s),
        ]

    def start_first(i):
        for copy in first_copies(i)[::-1]:
            start(copy)

    for i in range(min(AHEAD, chunks)):
        start_first(i)
    loads = [
        pltpu.make_async_copy(roots.at[0, 0], root_f32, local_sem.at[0]),
        pltpu.make_async_copy(grads.at[0, pl.ds(d_y * blocks, blocks)], mine_y, local_sem.at[1]),
        pltpu.make_async_copy(grads.at[0, pl.ds(d_x * blocks, blocks)], mine_x, local_sem.at[2]),
        pltpu.make_async_copy(grads.at[0, pl.ds(d * blocks, blocks)], mine, local_sem.at[3]),
    ]
    for copy in loads:
        copy.start()
    loads[0].wait()
    factors[core] = root_f32[...].astype(jnp.bfloat16)
    start(remote(factors.at[core], factors.at[core], factor_sems, 0, dp=d, shard=other))
    for copy in loads[1:]:
        copy.wait()

    def second_copy(i):
        far = d_y if i % 2 == 0 else d_x
        return remote(partial.at[i], second_own[i], second_sems, i, dp=far, shard=s)

    def pass_on(i):
        for copy in first_copies(i):
            copy.wait_recv()
        if i + AHEAD < chunks:
            start_first(i + AHEAD)
        held = mine_y if i % 2 == 0 else mine_x
        for b in range(blocks):
            total = held[b, pl.ds(i * SUB, SUB), :].astype(jnp.float32) + first_pass[i, b].astype(jnp.float32)
            partial[i, b] = total.astype(jnp.bfloat16)
        start(second_copy(i))

    def finish_sum(i):
        second_copy(i).wait_recv()
        for k in range(pairs):
            b = table[d, ahead(k)]
            total = mine[b, pl.ds(i * SUB, SUB), :].astype(jnp.float32) + first_own[i][b].astype(jnp.float32)
            total = (total + second_own[i][b].astype(jnp.float32)).astype(jnp.bfloat16)
            if k == 0:
                gradient[pl.ds(pl.multiple_of(s * rows + i * SUB, SUB), SUB), :] = total
            else:
                outgoing[i // 2, k - 1, pl.ds(i % 2 * SUB, SUB), :] = total

    def gradient_rows(owner, m):
        return gradient.at[pl.ds(pl.multiple_of(owner * rows + m * 2 * SUB, 2 * SUB), 2 * SUB), :]

    def block_copy(m, k):
        return remote(
            outgoing.at[m, k - 1],
            gradient_rows(s, m),
            block_sems,
            (m, k - 1),
            dp=d,
            shard=2 * ahead(k) + core,
        )

    def core_copy(m, k, owner):
        return remote(gradient_rows(owner, m), gradient_rows(owner, m), core_sems, (m, k), dp=d, shard=other)

    def start_blocks(m):
        for k in range(1, pairs):
            start(block_copy(m, k))
        start(core_copy(m, 0, s))

    def relay_blocks(m):
        for k in range(1, pairs):
            sender = 2 * behind(k) + core
            remote(outgoing.at[m, k - 1], gradient_rows(sender, m), block_sems, (m, k - 1), dp=d, shard=other).wait_recv()
            start(core_copy(m, k, sender))

    for i in range(chunks + LAG):
        if i < chunks:
            pass_on(i)
        j = i - LAG
        if j >= 0:
            finish_sum(j)
            if j % 2 == 1:
                start_blocks(j // 2)
                if j // 2 >= 1:
                    relay_blocks(j // 2 - 1)

    order = [0, pairs // 2] + [k for k in range(1, pairs) if k != pairs // 2]
    remote(factors.at[core], factors.at[1 - core], factor_sems, 0, dp=d, shard=other).wait_recv()
    for h in range(pieces):
        for n, k in enumerate(order):
            place = pl.multiple_of((2 * ahead(k) + core) * rows + h * PIECE, PIECE)
            left_rows[pl.ds((h * pairs + n) * PIECE, PIECE), :] = factors[0, pl.ds(place, PIECE), :]
    relay_blocks(rounds - 1)
    for m in range(rounds):
        for k in range(pairs):
            core_copy(m, k, 2 * behind(k) + 1 - core).wait_recv()

    def slot(replica, owner, h):
        return update_out.at[replica * pairs + owner, pl.ds(h * PIECE, PIECE), :]

    def start_gather(h, k, source):
        q = behind(k)
        start(remote(source, slot(d, q, h), gather_sems, (h, k, 0), dp=d_x, shard=s))
        start(remote(source, slot(d, q, h), gather_sems, (h, k, 1), dp=d_y, shard=s))

    def part(replica, k, h, side):
        return update_out.at[replica * pairs + behind(k), pl.ds(h * PIECE + side * half, half), :]

    def relay_updates(h, k):
        q = behind(k)
        for side, replica, to in ((0, d_x, d_y), (1, d_y, d_x)):
            remote(slot(replica, q, h), slot(replica, q, h), gather_sems, (h, k, side), dp=to, shard=s).wait_recv()
            mine_part = part(replica, k, h, side)
            start(remote(mine_part, mine_part, relay_sems, (h, k, side), dp=to, shard=s))

    def start_rows(h):
        for n, k in list(enumerate(order))[1:]:
            device = dict(dp=d, shard=2 * ahead(k) + core)
            start(remote(updates.at[h, n], slot(d, pair, h), row_sems, (h, k - 1), **device))

    per_step = max(1, min(pieces, 256 // (pairs * PIECE)))
    depth = pairs * PIECE
    own_copies = []
    for base in range(0, pieces, per_step):
        one_sided = jnp.dot(
            left_rows[pl.ds(base * depth, per_step * depth), :], gradient[...], preferred_element_type=jnp.float32
        ).astype(jnp.bfloat16)
        both = jnp.dot(one_sided, factors[1], preferred_element_type=jnp.float32).astype(jnp.bfloat16)
        for h in range(base, base + per_step):
            for n in range(pairs):
                place = ((h - base) * pairs + n) * PIECE
                updates[h, n] = both[place : place + PIECE]
            if h < ROWS_AHEAD:
                start_rows(h)
            start_gather(h, 0, updates.at[h, 0])
            own_copies.append(pltpu.make_async_copy(updates.at[h, 0], slot(d, pair, h), local_sem.at[4 + h]))
            own_copies[-1].start()

    tile = min(256, size)
    gram_copies = []

    def gram_tile(n):
        window = pl.ds(n * tile, tile)
        scale = (1.0 - keep_rate) / size

        @pl.when(core == 0)
        def _():
            product = lax.dot_general(
                gradient[window, :], gradient[...], (((1,), (1,)), ((), ())), preferred_element_type=jnp.float32
            )
            gram[window, :] = (scale * product).astype(jnp.bfloat16)

        @pl.when(core == 1)
        def _():
            product = jnp.dot(gradient[:, window].T, gradient[...], preferred_element_type=jnp.float32)
            gram[window, :] = (scale * product).astype(jnp.bfloat16)

        copy = pltpu.make_async_copy(gram.at[window, :], gram_out.at[window, :], gram_sem.at[n])
        copy.start()
        gram_copies.append(copy)

    tiles = list(range(size // tile))
    for h in range(pieces):
        relay_updates(h, 0)
    for h in range(pieces):
        for k in order[1:]:
            remote(updates.at[h, 0], slot(d, behind(k), h), row_sems, (h, k - 1), dp=d, shard=other).wait_recv()
            start_gather(h, k, slot(d, behind(k), h))
        if h + ROWS_AHEAD < pieces:
            start_rows(h + ROWS_AHEAD)
        if h >= 1:
            for k in order[1:]:
                relay_updates(h - 1, k)
        if tiles:
            gram_tile(tiles.pop(0))
    for k in order[1:]:
        relay_updates(pieces - 1, k)
    while tiles:
        gram_tile(tiles.pop(0))
    for h in range(pieces):
        for k in order:
            for side in range(2):
                far = part(d_z, k, h, side)
                remote(far, far, relay_sems, (h, k, side), dp=d_x, shard=s).wait_recv()
    for copy in own_copies:
        copy.wait()
    for copy in gram_copies:
        copy.wait()
    for copy in sent:
        copy.wait_send()


def exchange(table, grads, roots, pairs):
    _, total, rows, size = grads.shape
    blocks = total // 4
    chunks = rows // SUB
    rounds = chunks // 2
    pieces = rows // PIECE
    half = jnp.bfloat16
    dma = pltpu.SemaphoreType.DMA
    scratch = [pltpu.VMEM((blocks, SUB, size), half) for _ in range(2 * chunks)]
    scratch += [
        pltpu.VMEM((chunks, blocks, SUB, size), half),
        pltpu.VMEM((chunks, blocks, SUB, size), half),
        pltpu.VMEM((blocks, rows, size), half),
        pltpu.VMEM((blocks, rows, size), half),
        pltpu.VMEM((blocks, rows, size), half),
        pltpu.VMEM((rounds, pairs - 1, 2 * SUB, size), half),
        pltpu.VMEM((size, size), half),
        pltpu.VMEM((size, size), jnp.float32),
        pltpu.VMEM((2, size, size), half),
        pltpu.VMEM((pairs * rows, size), half),
        pltpu.VMEM((pieces, pairs, PIECE, size), half),
        pltpu.VMEM((size, size), half),
    ]
    shapes = [(chunks, 2), (chunks,), (rounds, pairs - 1), (rounds, pairs), (1,)]
    shapes += [(pieces, pairs - 1), (pieces, pairs, 2), (pieces, pairs, 2)]
    for shape in shapes:
        scratch += [dma(shape), dma(shape)]
    scratch += [dma((4 + pieces,)), dma((max(1, size // 256),))]
    return pl.pallas_call(
        functools.partial(exchange_kernel, pairs, blocks, rows, size),
        out_shape=(
            jax.ShapeDtypeStruct((total, rows, size), half),
            jax.ShapeDtypeStruct((size, size), half),
        ),
        in_specs=[
            pl.BlockSpec(memory_space=pltpu.SMEM),
            pl.BlockSpec(memory_space=pltpu.HBM),
            pl.BlockSpec(memory_space=pltpu.HBM),
        ],
        out_specs=[pl.BlockSpec(memory_space=pl.ANY)] * 2,
        scratch_shapes=scratch,
        compiler_params=pltpu.CompilerParams(
            collective_id=0, has_side_effects=True, vmem_limit_bytes=44 * 1024 * 1024
        ),
    )(table, grads, roots)


def finish_kernel(pairs, table, params, update, stats, gram, params_out, stats_out, new_params, new_stats, sems):
    total = params.shape[0]
    blocks = total // 4
    depth = stats.shape[0] // total
    copies = []
    for b in range(total):
        d, place = b // blocks, b % blocks
        found = jnp.int32(d * pairs)
        for p in range(pairs):
            found = found + jnp.where(table[d, p] == place, p, 0)
        stripe = pl.ds(b * depth, depth)
        new_stats[stripe, :] = keep_rate * stats[stripe, :] + gram[stripe, :].astype(jnp.float32)
        copies.append(pltpu.make_async_copy(new_stats.at[stripe, :], stats_out.at[stripe, :], sems.at[0, b]))
        copies[-1].start()
        moved = params[b].astype(jnp.float32) - step_size * update[found].astype(jnp.float32)
        new_params[b] = moved.astype(jnp.bfloat16)
        copies.append(pltpu.make_async_copy(new_params.at[b], params_out.at[b], sems.at[1, b]))
        copies[-1].start()
    for copy in copies:
        copy.wait()


def finish(table, params, update, stats, gram, pairs):
    return pl.pallas_call(
        functools.partial(finish_kernel, pairs),
        in_specs=[pl.BlockSpec(memory_space=pltpu.SMEM)] + [pl.BlockSpec(memory_space=pltpu.VMEM)] * 4,
        out_specs=[pl.BlockSpec(memory_space=pl.ANY)] * 2,
        out_shape=(
            jax.ShapeDtypeStruct(params.shape, jnp.bfloat16),
            jax.ShapeDtypeStruct(stats.shape, jnp.float32),
        ),
        scratch_shapes=[
            pltpu.VMEM(params.shape, jnp.bfloat16),
            pltpu.VMEM(stats.shape, jnp.float32),
            pltpu.SemaphoreType.DMA((2, params.shape[0])),
        ],
        compiler_params=pltpu.CompilerParams(vmem_limit_bytes=32 * 1024 * 1024),
    )(table, params, update, stats, gram)


def on_device(grads, params, stats, roots, table):
    pairs = lax.axis_size("shard") // 2
    update, gram = exchange(table, grads, roots, pairs)
    new_params, new_stats = finish(table, params, update, stats[0, 0], gram, pairs)
    return new_params, new_stats[None, None]


def solution(mesh):
    placed = (
        P("dp", None, "shard", None),
        P(None, "shard", None),
        P("dp", "shard", None, None),
        P("dp", "shard", None, None),
        P(),
    )
    return jax.shard_map(
        on_device,
        mesh=mesh,
        in_specs=placed,
        out_specs=(P(None, "shard", None), P("dp", "shard", None, None)),
        check_vma=False,
    )
```

```python
import functools

import jax
import jax.numpy as jnp
from jax import lax
from jax.experimental import pallas as pl
from jax.experimental.pallas import tpu as pltpu
from jax.sharding import PartitionSpec as P

keep_rate = 0.75
step_size = 0.25
SUB = 16
AHEAD = 4
LAG = 3
ROUND_LAG = 2
PIECE = 2 * SUB
ROWS_AHEAD = 3


def remote(src, dst, sems, index, **device):
    send_sem, recv_sem = sems
    return pltpu.make_async_remote_copy(
        src_ref=src,
        dst_ref=dst,
        send_sem=send_sem.at[index],
        recv_sem=recv_sem.at[index],
        device_id=device,
        device_id_type=pl.DeviceIdType.MESH,
    )


def exchange_kernel(pairs, blocks, rows, size, *refs):
    refs = list(refs)
    table, grads, roots, update_out, gram_out = refs[:5]
    refs = refs[5:]
    chunks = rows // SUB
    rounds = chunks
    pieces = rows // PIECE
    half = PIECE // 2
    first_own = [refs.pop(0) for _ in range(chunks)]
    second_own = [refs.pop(0) for _ in range(chunks)]
    (first_pass, partial, mine, mine_x, mine_y, outgoing, gradient, root_f32, factors, left_rows, updates, gram) = refs[:12]
    sems = refs[12:]
    first_sems, second_sems, block_sems, core_sems, factor_sems, row_sems, gather_sems, relay_sems = [
        (sems[2 * n], sems[2 * n + 1]) for n in range(8)
    ]
    local_sem, gram_sem = sems[16:18]

    d = lax.axis_index("dp")
    s = lax.axis_index("shard")
    pair = s // 2
    core = s % 2
    other = 2 * pair + 1 - core
    d_x = d + 1 - 2 * (d % 2)
    d_y = (d + 2) % 4
    d_z = 3 - d

    def ahead(k):
        return (pair + k) % pairs

    def behind(k):
        return (pair + pairs - k) % pairs

    barrier = pltpu.get_barrier_semaphore()
    greeted = [dict(dp=d_x, shard=s), dict(dp=d_y, shard=s), dict(dp=d, shard=other)]
    greeted += [dict(dp=d, shard=2 * ahead(k) + core) for k in range(1, pairs)]
    for device in greeted:
        pl.semaphore_signal(barrier, inc=1, device_id=device, device_id_type=pl.DeviceIdType.MESH)
    pl.semaphore_wait(barrier, len(greeted))

    sent = []

    def start(copy):
        copy.start()
        sent.append(copy)
        return copy

    def group(owner, i):
        return grads.at[0, pl.ds(owner * blocks, blocks), pl.ds(i * SUB, SUB), :]

    def first_copies(i):
        near = d_x if i % 2 == 0 else d_y
        return [
            remote(group(near, i), first_own[i], first_sems, (i, 0), dp=near, shard=s),
            remote(group(d_z, i), first_pass.at[i], first_sems, (i, 1), dp=near, shard=s),
        ]

    def start_first(i):
        for copy in first_copies(i)[::-1]:
            start(copy)

    for i in range(min(AHEAD, chunks)):
        start_first(i)
    loads = [
        pltpu.make_async_copy(roots.at[0, 0], root_f32, local_sem.at[0]),
        pltpu.make_async_copy(grads.at[0, pl.ds(d_y * blocks, blocks)], mine_y, local_sem.at[1]),
        pltpu.make_async_copy(grads.at[0, pl.ds(d_x * blocks, blocks)], mine_x, local_sem.at[2]),
        pltpu.make_async_copy(grads.at[0, pl.ds(d * blocks, blocks)], mine, local_sem.at[3]),
    ]
    for copy in loads:
        copy.start()
    loads[0].wait()
    factors[core] = root_f32[...].astype(jnp.bfloat16)
    start(remote(factors.at[core], factors.at[core], factor_sems, 0, dp=d, shard=other))
    for copy in loads[1:]:
        copy.wait()

    def second_copy(i):
        far = d_y if i % 2 == 0 else d_x
        return remote(partial.at[i], second_own[i], second_sems, i, dp=far, shard=s)

    def pass_on(i):
        for copy in first_copies(i):
            copy.wait_recv()
        if i + AHEAD < chunks:
            start_first(i + AHEAD)
        held = mine_y if i % 2 == 0 else mine_x
        for b in range(blocks):
            total = held[b, pl.ds(i * SUB, SUB), :].astype(jnp.float32) + first_pass[i, b].astype(jnp.float32)
            partial[i, b] = total.astype(jnp.bfloat16)
        start(second_copy(i))

    def finish_sum(i):
        second_copy(i).wait_recv()
        for k in range(pairs):
            b = table[d, ahead(k)]
            total = mine[b, pl.ds(i * SUB, SUB), :].astype(jnp.float32) + first_own[i][b].astype(jnp.float32)
            total = (total + second_own[i][b].astype(jnp.float32)).astype(jnp.bfloat16)
            if k == 0:
                gradient[pl.ds(pl.multiple_of(s * rows + i * SUB, SUB), SUB), :] = total
            else:
                outgoing[i, k - 1] = total

    def gradient_rows(owner, m):
        return gradient.at[pl.ds(pl.multiple_of(owner * rows + m * SUB, SUB), SUB), :]

    def block_copy(m, k):
        return remote(
            outgoing.at[m, k - 1],
            gradient_rows(s, m),
            block_sems,
            (m, k - 1),
            dp=d,
            shard=2 * ahead(k) + core,
        )

    def core_copy(m, k, owner):
        return remote(gradient_rows(owner, m), gradient_rows(owner, m), core_sems, (m, k), dp=d, shard=other)

    def start_blocks(m):
        for k in range(1, pairs):
            start(block_copy(m, k))
        start(core_copy(m, 0, s))

    def relay_blocks(m):
        for k in range(1, pairs):
            sender = 2 * behind(k) + core
            remote(outgoing.at[m, k - 1], gradient_rows(sender, m), block_sems, (m, k - 1), dp=d, shard=other).wait_recv()
            start(core_copy(m, k, sender))

    for i in range(chunks + LAG):
        if i < chunks:
            pass_on(i)
        j = i - LAG
        if j >= 0:
            finish_sum(j)
            start_blocks(j)
            if j >= ROUND_LAG:
                relay_blocks(j - ROUND_LAG)

    order = [0, pairs // 2] + [k for k in range(1, pairs) if k != pairs // 2]
    remote(factors.at[core], factors.at[1 - core], factor_sems, 0, dp=d, shard=other).wait_recv()
    for h in range(pieces):
        for n, k in enumerate(order):
            place = pl.multiple_of((2 * ahead(k) + core) * rows + h * PIECE, PIECE)
            left_rows[pl.ds((h * pairs + n) * PIECE, PIECE), :] = factors[0, pl.ds(place, PIECE), :]
    for m in range(max(0, rounds - ROUND_LAG), rounds):
        relay_blocks(m)
    for m in range(rounds):
        for k in range(pairs):
            core_copy(m, k, 2 * behind(k) + 1 - core).wait_recv()

    def slot(replica, owner, h):
        return update_out.at[replica * pairs + owner, pl.ds(h * PIECE, PIECE), :]

    def start_gather(h, k, source):
        q = behind(k)
        start(remote(source, slot(d, q, h), gather_sems, (h, k, 0), dp=d_x, shard=s))
        start(remote(source, slot(d, q, h), gather_sems, (h, k, 1), dp=d_y, shard=s))

    def part(replica, k, h, side):
        return update_out.at[replica * pairs + behind(k), pl.ds(h * PIECE + side * half, half), :]

    def relay_updates(h, k):
        q = behind(k)
        for side, replica, to in ((0, d_x, d_y), (1, d_y, d_x)):
            remote(slot(replica, q, h), slot(replica, q, h), gather_sems, (h, k, side), dp=to, shard=s).wait_recv()
            mine_part = part(replica, k, h, side)
            start(remote(mine_part, mine_part, relay_sems, (h, k, side), dp=to, shard=s))

    def start_rows(h):
        for n, k in list(enumerate(order))[1:]:
            device = dict(dp=d, shard=2 * ahead(k) + core)
            start(remote(updates.at[h, n], slot(d, pair, h), row_sems, (h, k - 1), **device))

    per_step = max(1, min(pieces, 256 // (pairs * PIECE)))
    depth = pairs * PIECE
    own_copies = []
    for base in range(0, pieces, per_step):
        one_sided = jnp.dot(
            left_rows[pl.ds(base * depth, per_step * depth), :], gradient[...], preferred_element_type=jnp.float32
        ).astype(jnp.bfloat16)
        both = jnp.dot(one_sided, factors[1], preferred_element_type=jnp.float32).astype(jnp.bfloat16)
        for h in range(base, base + per_step):
            for n in range(pairs):
                place = ((h - base) * pairs + n) * PIECE
                updates[h, n] = both[place : place + PIECE]
            if h < ROWS_AHEAD:
                start_rows(h)
            start_gather(h, 0, updates.at[h, 0])
            own_copies.append(pltpu.make_async_copy(updates.at[h, 0], slot(d, pair, h), local_sem.at[4 + h]))
            own_copies[-1].start()

    tile = min(256, size)
    gram_copies = []

    def gram_tile(n):
        window = pl.ds(n * tile, tile)
        scale = (1.0 - keep_rate) / size

        @pl.when(core == 0)
        def _():
            product = lax.dot_general(
                gradient[window, :], gradient[...], (((1,), (1,)), ((), ())), preferred_element_type=jnp.float32
            )
            gram[window, :] = (scale * product).astype(jnp.bfloat16)

        @pl.when(core == 1)
        def _():
            product = jnp.dot(gradient[:, window].T, gradient[...], preferred_element_type=jnp.float32)
            gram[window, :] = (scale * product).astype(jnp.bfloat16)

        copy = pltpu.make_async_copy(gram.at[window, :], gram_out.at[window, :], gram_sem.at[n])
        copy.start()
        gram_copies.append(copy)

    tiles = list(range(size // tile))
    for h in range(pieces):
        relay_updates(h, 0)
    for h in range(pieces):
        for k in order[1:]:
            remote(updates.at[h, 0], slot(d, behind(k), h), row_sems, (h, k - 1), dp=d, shard=other).wait_recv()
            start_gather(h, k, slot(d, behind(k), h))
        if h + ROWS_AHEAD < pieces:
            start_rows(h + ROWS_AHEAD)
        if h >= 1:
            for k in order[1:]:
                relay_updates(h - 1, k)
        if tiles:
            gram_tile(tiles.pop(0))
    for k in order[1:]:
        relay_updates(pieces - 1, k)
    while tiles:
        gram_tile(tiles.pop(0))
    for h in range(pieces):
        for k in order:
            for side in range(2):
                far = part(d_z, k, h, side)
                remote(far, far, relay_sems, (h, k, side), dp=d_x, shard=s).wait_recv()
    for copy in own_copies:
        copy.wait()
    for copy in gram_copies:
        copy.wait()
    for copy in sent:
        copy.wait_send()


def exchange(table, grads, roots, pairs):
    _, total, rows, size = grads.shape
    blocks = total // 4
    chunks = rows // SUB
    rounds = chunks
    pieces = rows // PIECE
    half = jnp.bfloat16
    dma = pltpu.SemaphoreType.DMA
    scratch = [pltpu.VMEM((blocks, SUB, size), half) for _ in range(2 * chunks)]
    scratch += [
        pltpu.VMEM((chunks, blocks, SUB, size), half),
        pltpu.VMEM((chunks, blocks, SUB, size), half),
        pltpu.VMEM((blocks, rows, size), half),
        pltpu.VMEM((blocks, rows, size), half),
        pltpu.VMEM((blocks, rows, size), half),
        pltpu.VMEM((rounds, pairs - 1, SUB, size), half),
        pltpu.VMEM((size, size), half),
        pltpu.VMEM((size, size), jnp.float32),
        pltpu.VMEM((2, size, size), half),
        pltpu.VMEM((pairs * rows, size), half),
        pltpu.VMEM((pieces, pairs, PIECE, size), half),
        pltpu.VMEM((size, size), half),
    ]
    shapes = [(chunks, 2), (chunks,), (rounds, pairs - 1), (rounds, pairs), (1,)]
    shapes += [(pieces, pairs - 1), (pieces, pairs, 2), (pieces, pairs, 2)]
    for shape in shapes:
        scratch += [dma(shape), dma(shape)]
    scratch += [dma((4 + pieces,)), dma((max(1, size // 256),))]
    return pl.pallas_call(
        functools.partial(exchange_kernel, pairs, blocks, rows, size),
        out_shape=(
            jax.ShapeDtypeStruct((total, rows, size), half),
            jax.ShapeDtypeStruct((size, size), half),
        ),
        in_specs=[
            pl.BlockSpec(memory_space=pltpu.SMEM),
            pl.BlockSpec(memory_space=pltpu.HBM),
            pl.BlockSpec(memory_space=pltpu.HBM),
        ],
        out_specs=[pl.BlockSpec(memory_space=pl.ANY)] * 2,
        scratch_shapes=scratch,
        compiler_params=pltpu.CompilerParams(
            collective_id=0, has_side_effects=True, vmem_limit_bytes=44 * 1024 * 1024
        ),
    )(table, grads, roots)


def finish_kernel(pairs, table, params, update, stats, gram, params_out, stats_out, new_params, new_stats, sems):
    total = params.shape[0]
    blocks = total // 4
    depth = stats.shape[0] // total
    copies = []
    for b in range(total):
        d, place = b // blocks, b % blocks
        found = jnp.int32(d * pairs)
        for p in range(pairs):
            found = found + jnp.where(table[d, p] == place, p, 0)
        stripe = pl.ds(b * depth, depth)
        new_stats[stripe, :] = keep_rate * stats[stripe, :] + gram[stripe, :].astype(jnp.float32)
        copies.append(pltpu.make_async_copy(new_stats.at[stripe, :], stats_out.at[stripe, :], sems.at[0, b]))
        copies[-1].start()
        moved = params[b].astype(jnp.float32) - step_size * update[found].astype(jnp.float32)
        new_params[b] = moved.astype(jnp.bfloat16)
        copies.append(pltpu.make_async_copy(new_params.at[b], params_out.at[b], sems.at[1, b]))
        copies[-1].start()
    for copy in copies:
        copy.wait()


def finish(table, params, update, stats, gram, pairs):
    return pl.pallas_call(
        functools.partial(finish_kernel, pairs),
        in_specs=[pl.BlockSpec(memory_space=pltpu.SMEM)] + [pl.BlockSpec(memory_space=pltpu.VMEM)] * 4,
        out_specs=[pl.BlockSpec(memory_space=pl.ANY)] * 2,
        out_shape=(
            jax.ShapeDtypeStruct(params.shape, jnp.bfloat16),
            jax.ShapeDtypeStruct(stats.shape, jnp.float32),
        ),
        scratch_shapes=[
            pltpu.VMEM(params.shape, jnp.bfloat16),
            pltpu.VMEM(stats.shape, jnp.float32),
            pltpu.SemaphoreType.DMA((2, params.shape[0])),
        ],
        compiler_params=pltpu.CompilerParams(vmem_limit_bytes=32 * 1024 * 1024),
    )(table, params, update, stats, gram)


def on_device(grads, params, stats, roots, table):
    pairs = lax.axis_size("shard") // 2
    update, gram = exchange(table, grads, roots, pairs)
    new_params, new_stats = finish(table, params, update, stats[0, 0], gram, pairs)
    return new_params, new_stats[None, None]


def solution(mesh):
    placed = (
        P("dp", None, "shard", None),
        P(None, "shard", None),
        P("dp", "shard", None, None),
        P("dp", "shard", None, None),
        P(),
    )
    return jax.shard_map(
        on_device,
        mesh=mesh,
        in_specs=placed,
        out_specs=(P(None, "shard", None), P("dp", "shard", None, None)),
        check_vma=False,
    )
```

```python
import functools

import jax
import jax.numpy as jnp
from jax import lax
from jax.experimental import pallas as pl
from jax.experimental.pallas import tpu as pltpu
from jax.sharding import PartitionSpec as P

keep_rate = 0.75
step_size = 0.25
SUB = 16
AHEAD = 6
LAG = 3
PIECE = 2 * SUB
ROWS_AHEAD = 3


def remote(src, dst, sems, index, **device):
    send_sem, recv_sem = sems
    return pltpu.make_async_remote_copy(
        src_ref=src,
        dst_ref=dst,
        send_sem=send_sem.at[index],
        recv_sem=recv_sem.at[index],
        device_id=device,
        device_id_type=pl.DeviceIdType.MESH,
    )


def exchange_kernel(pairs, blocks, rows, size, *refs):
    refs = list(refs)
    table, grads, roots, update_out, gram_out = refs[:5]
    refs = refs[5:]
    chunks = rows // SUB
    rounds = chunks // 2
    pieces = rows // PIECE
    half = PIECE // 2
    first_own = [refs.pop(0) for _ in range(chunks)]
    second_own = [refs.pop(0) for _ in range(chunks)]
    (first_pass, partial, mine, mine_x, mine_y, outgoing, gradient, root_f32, factors, left_rows, updates, gram) = refs[:12]
    sems = refs[12:]
    first_sems, second_sems, block_sems, core_sems, factor_sems, row_sems, gather_sems, relay_sems = [
        (sems[2 * n], sems[2 * n + 1]) for n in range(8)
    ]
    local_sem, gram_sem = sems[16:18]

    d = lax.axis_index("dp")
    s = lax.axis_index("shard")
    pair = s // 2
    core = s % 2
    other = 2 * pair + 1 - core
    d_x = d + 1 - 2 * (d % 2)
    d_y = (d + 2) % 4
    d_z = 3 - d

    def ahead(k):
        return (pair + k) % pairs

    def behind(k):
        return (pair + pairs - k) % pairs

    barrier = pltpu.get_barrier_semaphore()
    greeted = [dict(dp=d_x, shard=s), dict(dp=d_y, shard=s), dict(dp=d, shard=other)]
    greeted += [dict(dp=d, shard=2 * ahead(k) + core) for k in range(1, pairs)]
    for device in greeted:
        pl.semaphore_signal(barrier, inc=1, device_id=device, device_id_type=pl.DeviceIdType.MESH)
    pl.semaphore_wait(barrier, len(greeted))

    sent = []

    def start(copy):
        copy.start()
        sent.append(copy)
        return copy

    def group(owner, i):
        return grads.at[0, pl.ds(owner * blocks, blocks), pl.ds(i * SUB, SUB), :]

    def first_copies(i):
        near = d_x if i % 2 == 0 else d_y
        return [
            remote(group(near, i), first_own[i], first_sems, (i, 0), dp=near, shard=s),
            remote(group(d_z, i), first_pass.at[i], first_sems, (i, 1), dp=near, shard=s),
        ]

    def start_first(i):
        for copy in first_copies(i)[::-1]:
            start(copy)

    for i in range(min(AHEAD, chunks)):
        start_first(i)
    loads = [
        pltpu.make_async_copy(roots.at[0, 0], root_f32, local_sem.at[0]),
        pltpu.make_async_copy(grads.at[0, pl.ds(d_y * blocks, blocks)], mine_y, local_sem.at[1]),
        pltpu.make_async_copy(grads.at[0, pl.ds(d_x * blocks, blocks)], mine_x, local_sem.at[2]),
        pltpu.make_async_copy(grads.at[0, pl.ds(d * blocks, blocks)], mine, local_sem.at[3]),
    ]
    for copy in loads:
        copy.start()
    loads[0].wait()
    factors[core] = root_f32[...].astype(jnp.bfloat16)
    start(remote(factors.at[core], factors.at[core], factor_sems, 0, dp=d, shard=other))
    for copy in loads[1:]:
        copy.wait()

    def second_copy(i):
        far = d_y if i % 2 == 0 else d_x
        return remote(partial.at[i], second_own[i], second_sems, i, dp=far, shard=s)

    def pass_on(i):
        for copy in first_copies(i):
            copy.wait_recv()
        if i + AHEAD < chunks:
            start_first(i + AHEAD)
        held = mine_y if i % 2 == 0 else mine_x
        for b in range(blocks):
            total = held[b, pl.ds(i * SUB, SUB), :].astype(jnp.float32) + first_pass[i, b].astype(jnp.float32)
            partial[i, b] = total.astype(jnp.bfloat16)
        start(second_copy(i))

    def finish_sum(i):
        second_copy(i).wait_recv()
        for k in range(pairs):
            b = table[d, ahead(k)]
            total = mine[b, pl.ds(i * SUB, SUB), :].astype(jnp.float32) + first_own[i][b].astype(jnp.float32)
            total = (total + second_own[i][b].astype(jnp.float32)).astype(jnp.bfloat16)
            if k == 0:
                gradient[pl.ds(pl.multiple_of(s * rows + i * SUB, SUB), SUB), :] = total
            else:
                outgoing[i // 2, k - 1, pl.ds(i % 2 * SUB, SUB), :] = total

    def gradient_rows(owner, m):
        return gradient.at[pl.ds(pl.multiple_of(owner * rows + m * 2 * SUB, 2 * SUB), 2 * SUB), :]

    def block_copy(m, k):
        return remote(
            outgoing.at[m, k - 1],
            gradient_rows(s, m),
            block_sems,
            (m, k - 1),
            dp=d,
            shard=2 * ahead(k) + core,
        )

    def core_copy(m, k, owner):
        return remote(gradient_rows(owner, m), gradient_rows(owner, m), core_sems, (m, k), dp=d, shard=other)

    def start_blocks(m):
        for k in range(1, pairs):
            start(block_copy(m, k))
        start(core_copy(m, 0, s))

    def relay_blocks(m):
        for k in range(1, pairs):
            sender = 2 * behind(k) + core
            remote(outgoing.at[m, k - 1], gradient_rows(sender, m), block_sems, (m, k - 1), dp=d, shard=other).wait_recv()
            start(core_copy(m, k, sender))

    for i in range(chunks + LAG):
        if i < chunks:
            pass_on(i)
        j = i - LAG
        if j >= 0:
            finish_sum(j)
            if j % 2 == 1:
                start_blocks(j // 2)
                if j // 2 >= 1:
                    relay_blocks(j // 2 - 1)

    order = [0, pairs // 2] + [k for k in range(1, pairs) if k != pairs // 2]
    remote(factors.at[core], factors.at[1 - core], factor_sems, 0, dp=d, shard=other).wait_recv()
    for h in range(pieces):
        for n, k in enumerate(order):
            place = pl.multiple_of((2 * ahead(k) + core) * rows + h * PIECE, PIECE)
            left_rows[pl.ds((h * pairs + n) * PIECE, PIECE), :] = factors[0, pl.ds(place, PIECE), :]
    relay_blocks(rounds - 1)
    for m in range(rounds):
        for k in range(pairs):
            core_copy(m, k, 2 * behind(k) + 1 - core).wait_recv()

    def slot(replica, owner, h):
        return update_out.at[replica * pairs + owner, pl.ds(h * PIECE, PIECE), :]

    def start_gather(h, k, source):
        q = behind(k)
        start(remote(source, slot(d, q, h), gather_sems, (h, k, 0), dp=d_x, shard=s))
        start(remote(source, slot(d, q, h), gather_sems, (h, k, 1), dp=d_y, shard=s))

    def part(replica, k, h, side):
        return update_out.at[replica * pairs + behind(k), pl.ds(h * PIECE + side * half, half), :]

    def relay_updates(h, k):
        q = behind(k)
        for side, replica, to in ((0, d_x, d_y), (1, d_y, d_x)):
            remote(slot(replica, q, h), slot(replica, q, h), gather_sems, (h, k, side), dp=to, shard=s).wait_recv()
            mine_part = part(replica, k, h, side)
            start(remote(mine_part, mine_part, relay_sems, (h, k, side), dp=to, shard=s))

    def start_rows(h):
        for n, k in list(enumerate(order))[1:]:
            device = dict(dp=d, shard=2 * ahead(k) + core)
            start(remote(updates.at[h, n], slot(d, pair, h), row_sems, (h, k - 1), **device))

    per_step = max(1, min(pieces, 256 // (pairs * PIECE)))
    depth = pairs * PIECE
    own_copies = []
    for base in range(0, pieces, per_step):
        one_sided = jnp.dot(
            left_rows[pl.ds(base * depth, per_step * depth), :], gradient[...], preferred_element_type=jnp.float32
        ).astype(jnp.bfloat16)
        both = jnp.dot(one_sided, factors[1], preferred_element_type=jnp.float32).astype(jnp.bfloat16)
        for h in range(base, base + per_step):
            for n in range(pairs):
                place = ((h - base) * pairs + n) * PIECE
                updates[h, n] = both[place : place + PIECE]
            if h < ROWS_AHEAD:
                start_rows(h)
            start_gather(h, 0, updates.at[h, 0])
            own_copies.append(pltpu.make_async_copy(updates.at[h, 0], slot(d, pair, h), local_sem.at[4 + h]))
            own_copies[-1].start()

    tile = min(256, size)
    gram_copies = []

    def gram_tile(n):
        window = pl.ds(n * tile, tile)
        scale = (1.0 - keep_rate) / size

        @pl.when(core == 0)
        def _():
            product = lax.dot_general(
                gradient[window, :], gradient[...], (((1,), (1,)), ((), ())), preferred_element_type=jnp.float32
            )
            gram[window, :] = (scale * product).astype(jnp.bfloat16)

        @pl.when(core == 1)
        def _():
            product = jnp.dot(gradient[:, window].T, gradient[...], preferred_element_type=jnp.float32)
            gram[window, :] = (scale * product).astype(jnp.bfloat16)

        copy = pltpu.make_async_copy(gram.at[window, :], gram_out.at[window, :], gram_sem.at[n])
        copy.start()
        gram_copies.append(copy)

    tiles = list(range(size // tile))
    for h in range(pieces):
        relay_updates(h, 0)
    for h in range(pieces):
        for k in order[1:]:
            remote(updates.at[h, 0], slot(d, behind(k), h), row_sems, (h, k - 1), dp=d, shard=other).wait_recv()
            start_gather(h, k, slot(d, behind(k), h))
        if h + ROWS_AHEAD < pieces:
            start_rows(h + ROWS_AHEAD)
        if h >= 1:
            for k in order[1:]:
                relay_updates(h - 1, k)
        if tiles:
            gram_tile(tiles.pop(0))
    for k in order[1:]:
        relay_updates(pieces - 1, k)
    while tiles:
        gram_tile(tiles.pop(0))
    for h in range(pieces):
        for k in order:
            for side in range(2):
                far = part(d_z, k, h, side)
                remote(far, far, relay_sems, (h, k, side), dp=d_x, shard=s).wait_recv()
    for copy in own_copies:
        copy.wait()
    for copy in gram_copies:
        copy.wait()
    for copy in sent:
        copy.wait_send()


def exchange(table, grads, roots, pairs):
    _, total, rows, size = grads.shape
    blocks = total // 4
    chunks = rows // SUB
    rounds = chunks // 2
    pieces = rows // PIECE
    half = jnp.bfloat16
    dma = pltpu.SemaphoreType.DMA
    scratch = [pltpu.VMEM((blocks, SUB, size), half) for _ in range(2 * chunks)]
    scratch += [
        pltpu.VMEM((chunks, blocks, SUB, size), half),
        pltpu.VMEM((chunks, blocks, SUB, size), half),
        pltpu.VMEM((blocks, rows, size), half),
        pltpu.VMEM((blocks, rows, size), half),
        pltpu.VMEM((blocks, rows, size), half),
        pltpu.VMEM((rounds, pairs - 1, 2 * SUB, size), half),
        pltpu.VMEM((size, size), half),
        pltpu.VMEM((size, size), jnp.float32),
        pltpu.VMEM((2, size, size), half),
        pltpu.VMEM((pairs * rows, size), half),
        pltpu.VMEM((pieces, pairs, PIECE, size), half),
        pltpu.VMEM((size, size), half),
    ]
    shapes = [(chunks, 2), (chunks,), (rounds, pairs - 1), (rounds, pairs), (1,)]
    shapes += [(pieces, pairs - 1), (pieces, pairs, 2), (pieces, pairs, 2)]
    for shape in shapes:
        scratch += [dma(shape), dma(shape)]
    scratch += [dma((4 + pieces,)), dma((max(1, size // 256),))]
    return pl.pallas_call(
        functools.partial(exchange_kernel, pairs, blocks, rows, size),
        out_shape=(
            jax.ShapeDtypeStruct((total, rows, size), half),
            jax.ShapeDtypeStruct((size, size), half),
        ),
        in_specs=[
            pl.BlockSpec(memory_space=pltpu.SMEM),
            pl.BlockSpec(memory_space=pltpu.HBM),
            pl.BlockSpec(memory_space=pltpu.HBM),
        ],
        out_specs=[pl.BlockSpec(memory_space=pl.ANY)] * 2,
        scratch_shapes=scratch,
        compiler_params=pltpu.CompilerParams(
            collective_id=0, has_side_effects=True, vmem_limit_bytes=44 * 1024 * 1024
        ),
    )(table, grads, roots)


def finish_kernel(pairs, table, params, update, stats, gram, params_out, stats_out, new_params, new_stats, sems):
    total = params.shape[0]
    blocks = total // 4
    depth = stats.shape[0] // total
    copies = []
    for b in range(total):
        d, place = b // blocks, b % blocks
        found = jnp.int32(d * pairs)
        for p in range(pairs):
            found = found + jnp.where(table[d, p] == place, p, 0)
        stripe = pl.ds(b * depth, depth)
        new_stats[stripe, :] = keep_rate * stats[stripe, :] + gram[stripe, :].astype(jnp.float32)
        copies.append(pltpu.make_async_copy(new_stats.at[stripe, :], stats_out.at[stripe, :], sems.at[0, b]))
        copies[-1].start()
        moved = params[b].astype(jnp.float32) - step_size * update[found].astype(jnp.float32)
        new_params[b] = moved.astype(jnp.bfloat16)
        copies.append(pltpu.make_async_copy(new_params.at[b], params_out.at[b], sems.at[1, b]))
        copies[-1].start()
    for copy in copies:
        copy.wait()


def finish(table, params, update, stats, gram, pairs):
    return pl.pallas_call(
        functools.partial(finish_kernel, pairs),
        in_specs=[pl.BlockSpec(memory_space=pltpu.SMEM)] + [pl.BlockSpec(memory_space=pltpu.VMEM)] * 4,
        out_specs=[pl.BlockSpec(memory_space=pl.ANY)] * 2,
        out_shape=(
            jax.ShapeDtypeStruct(params.shape, jnp.bfloat16),
            jax.ShapeDtypeStruct(stats.shape, jnp.float32),
        ),
        scratch_shapes=[
            pltpu.VMEM(params.shape, jnp.bfloat16),
            pltpu.VMEM(stats.shape, jnp.float32),
            pltpu.SemaphoreType.DMA((2, params.shape[0])),
        ],
        compiler_params=pltpu.CompilerParams(vmem_limit_bytes=32 * 1024 * 1024),
    )(table, params, update, stats, gram)


def on_device(grads, params, stats, roots, table):
    pairs = lax.axis_size("shard") // 2
    update, gram = exchange(table, grads, roots, pairs)
    new_params, new_stats = finish(table, params, update, stats[0, 0], gram, pairs)
    return new_params, new_stats[None, None]


def solution(mesh):
    placed = (
        P("dp", None, "shard", None),
        P(None, "shard", None),
        P("dp", "shard", None, None),
        P("dp", "shard", None, None),
        P(),
    )
    return jax.shard_map(
        on_device,
        mesh=mesh,
        in_specs=placed,
        out_specs=(P(None, "shard", None), P("dp", "shard", None, None)),
        check_vma=False,
    )
```
